32 devices in a mesh: group: 2 (over y), section: 4 (over z), dp: 4 (over x, core).
Axes of the slice: x: 2, y: 2, z: 4, core: 2. Of those that a mesh axis runs over, the one named last changes fastest.
Arguments:
- tokens: bfloat16 [4, 8, 32, 1600], P(None, ('group', 'dp')), parts along dimension 1, may hold values from -6 to 6
- pixel_index: int32 [4, 8, 384], P(None, ('group', 'dp')), parts along dimension 1, may hold values from 0 to 6271
- point_mask: int32 [4, 8, 384], P(None, ('group', 'dp')), parts along dimension 1, may hold values from 0 to 1, as said below
- point_depth: float32 [4, 8, 384], P(None, ('group', 'dp')), parts along dimension 1, may hold values from -6 to 6
- hook_section: int32 [4], replicated, may hold values from 0 to 2, as said below
- w_query: bfloat16 [4, 1600, 832], P('section')
- w_key: bfloat16 [4, 1600, 832], P('section')
- w_value: bfloat16 [4, 1600, 832], P('section'), may hold values from -0.15625 to 0.15625
- w_output: bfloat16 [4, 832, 1600], P('section'), may hold values from -0.21875 to 0.21875
- reassemble: bfloat16 [5, 1600, 128], P(None, None, ('section', 'dp')), may hold values from -0.15625 to 0.15625
- merging: bfloat16 [4, 128, 128], P(None, None, ('section', 'dp')), may hold values from -0.5 to 0.5
- predict: bfloat16 [128, 196], P(('section', 'dp')), may hold values from -0.5 to 0.5
Outputs:
- grad_query: bfloat16 [8, 1600, 832], P(('group', 'section'), 'dp'), parts along dimension 0
- grad_key: bfloat16 [8, 1600, 832], P(('group', 'section'), 'dp'), parts along dimension 0
- grad_value: bfloat16 [8, 1600, 832], P(('group', 'section'), 'dp'), parts along dimension 0
- grad_output: bfloat16 [8, 832, 1600], P(('group', 'section'), 'dp'), parts along dimension 0
- grad_reassemble: float32 [10, 1600, 128], P('group', None, ('section', 'dp')), parts along dimension 0
- grad_merging: float32 [8, 128, 128], P('group', None, ('section', 'dp')), parts along dimension 0
- grad_predict: float32 [256, 196], P(('group', 'section', 'dp')), parts along dimension 0
The draws below stay inside these ranges and needn't reach their ends.
There are 2 independent parts, one for each index of `group`. The reference program is written for one: setup_inputs(seed, part) draws one part's arguments, and reference() takes and returns one part's arrays. A program takes and returns all parts, laid end to end along the dimension named above; an argument that names none is the same for every part. Nothing has to cross between parts.
Inputs may be any that keep to these rules, and one draw needn't show every extreme that they name: `point_mask`: in each image the valid points come first, and at least 48 of them are valid. `hook_section`: Sorted; the last entry is 2.
All inputs are finite; a program needn't handle non-finite values.
Results may differ from the reference program's by a relative error of at most 0.03.
Values may be sent and summed in bfloat16 or wider, within the bound.
A program may use at most 128 MiB of HBM per device.

```python
import math
import jax
import jax.numpy as jnp
from jax import lax

D = 1600
HEADS = 13
HSZ = 64
F = 128
PIX = 196
L = 32
MB = 4
NPTS = 384
NHOOK = 4
IMG_DEV = 1
NSTG = 4
HD = 832
IMAGES = 4
N_DP = 4


def drawn_weight(key, salt_value):
    own_part = jax.random.normal(jax.random.fold_in(key, salt_value), (NSTG, D, HEADS, HSZ), jnp.float32)
    return (own_part * D ** (-0.5)).reshape(NSTG, D, HEADS * HSZ).astype(jnp.bfloat16)


def draw_w_query(key, part):
    return drawn_weight(key, 1)


def draw_w_key(key, part):
    return drawn_weight(key, 2)


def draw_point_mask(key, part):
    valid_count = jax.random.randint(jax.random.fold_in(key, 5), (MB, IMAGES, 1), NPTS // 8, NPTS + 1)
    position = lax.broadcasted_iota(jnp.int32, (MB, IMAGES, NPTS), 2)
    return (position < valid_count).astype(jnp.int32)


def draw_hook_section(key, part):
    earlier = jnp.sort(jax.random.randint(jax.random.fold_in(key, 9), (NHOOK - 1,), 0, NSTG - 1))
    deepest = jnp.full((1,), NSTG - 2, jnp.int32)
    return jnp.concatenate([earlier.astype(jnp.int32), deepest]).astype(jnp.int32)


def with_ends(drawn, own_key, least, top_value):
    longest = drawn.shape.index(max(drawn.shape))
    spots = []
    for shift in (0, 1):
        where = [jax.random.randint(jax.random.fold_in(own_key, axis), (), 0, length) for axis, length in enumerate(drawn.shape)]
        where[longest] = (where[longest] + shift) % drawn.shape[longest]
        spots.append(tuple(where))
    return drawn.at[spots[0]].set(least).at[spots[1]].set(top_value)


def levels(rng, extent, shards, least, largest):
    gain = 1.0
    for dim, shards_of in shards:
        draws = jax.random.uniform(jax.random.fold_in(jax.random.fold_in(rng, 6), dim), (shards_of,), jnp.float32, least / len(shards), largest / len(shards))
        gain = gain * jnp.repeat(jnp.exp(draws), extent[dim] // shards_of).reshape((-1,) + (1,) * (len(extent) - 1 - dim))
    return gain


def scatter_about(rng, shape, width, reach, pieces=(), held_as=jnp.bfloat16):
    entries = jax.random.normal(rng, shape, jnp.float32) * width
    if len(pieces) > 0:
        entries = levels(rng, shape, pieces, -0.22, 0.18) * entries
    return jnp.clip(entries, min=-reach, max=reach).astype(held_as)


def setup_inputs(seed: int = 0, part: int = 0) -> dict:
    seeds = jax.random.split(jax.random.key(seed), 13)
    part_splits = jax.random.split(jax.random.fold_in(seeds[12], part), 13)
    tokens = scatter_about(part_splits[0], (MB, IMAGES, L, D), 1.0, 6.0, ((1, 4),))
    pixel_index = with_ends(jax.random.randint(part_splits[1], (MB, IMAGES, NPTS), 0, L * PIX), jax.random.fold_in(part_splits[1], 1), 0, (L * PIX) - 1).astype(jnp.int32)
    point_mask = draw_point_mask(jax.random.fold_in(jax.random.fold_in(seeds[12], part), 71), part)
    point_depth = scatter_about(part_splits[3], (MB, IMAGES, NPTS), 1.0, 6.0, ((1, 4),), jnp.float32)
    hook_section = draw_hook_section(jax.random.fold_in(seeds[12], 71), part)
    w_query = draw_w_query(jax.random.fold_in(seeds[12], 71), part)
    w_key = draw_w_key(jax.random.fold_in(seeds[12], 71), part)
    w_value = scatter_about(seeds[7], (NSTG, D, HD), D ** -0.5, 0.15625, ((0, 4),))
    w_output = scatter_about(seeds[8], (NSTG, HD, D), HD ** -0.5, 0.21875, ((0, 4),))
    reassemble = scatter_about(seeds[9], (NHOOK + 1, D, F), D ** -0.5, 0.15625, ((2, 16),))
    merging = scatter_about(seeds[10], (NHOOK, F, F), F ** -0.5, 0.5, ((2, 16),))
    predict = scatter_about(seeds[11], (F, PIX), F ** -0.5, 0.5, ((0, 16),))
    return dict(tokens=tokens, pixel_index=pixel_index, point_mask=point_mask, point_depth=point_depth, hook_section=hook_section, w_query=w_query, w_key=w_key, w_value=w_value, w_output=w_output, reassemble=reassemble, merging=merging, predict=predict)


EPS = 1e-06

def rms_normed(stream):
    widened = stream.astype(jnp.float32)
    inv_root = lax.rsqrt(lax.optimization_barrier(jnp.mean(widened * widened, axis=-1, keepdims=True)) + EPS)
    return (widened * inv_root).astype(jnp.bfloat16)

def attend(query_rows, key_rows, value_rows):
    image_count, token_count, inner_width = query_rows.shape
    head_width = inner_width // HEADS
    shape_heads = (image_count, token_count, HEADS, head_width)
    query_heads = query_rows.astype(jnp.float32).reshape(shape_heads)
    key_heads = key_rows.astype(jnp.float32).reshape(shape_heads)
    value_heads = value_rows.astype(jnp.float32).reshape(shape_heads)
    scores = jnp.einsum('bqhe,bkhe->bhqk', query_heads, key_heads) / math.sqrt(head_width)
    probabilities = jax.nn.softmax(scores, axis=-1).astype(jnp.bfloat16)
    mixed_heads = jnp.einsum('bhqk,bkhe->bqhe', probabilities.astype(jnp.float32), value_heads)
    return mixed_heads.reshape(image_count, token_count, inner_width).astype(jnp.bfloat16)

def attention_layer(stream, layer_query, layer_key, layer_value, layer_output, nudges):
    image_count, token_count, model_width = stream.shape
    normed = rms_normed(stream).reshape(image_count * token_count, model_width)
    query_rows = jnp.dot(normed, layer_query, preferred_element_type=jnp.float32).astype(jnp.bfloat16) + nudges[0]
    key_rows = jnp.dot(normed, layer_key, preferred_element_type=jnp.float32).astype(jnp.bfloat16) + nudges[1]
    value_rows = jnp.dot(normed, layer_value, preferred_element_type=jnp.float32).astype(jnp.bfloat16) + nudges[2]
    inner_width = layer_query.shape[1]
    mixed = attend(query_rows.reshape(image_count, token_count, inner_width), key_rows.reshape(image_count, token_count, inner_width), value_rows.reshape(image_count, token_count, inner_width))
    mixed_rows = mixed.reshape(image_count * token_count, inner_width)
    update = jnp.dot(mixed_rows, layer_output, preferred_element_type=jnp.float32)
    update = update.reshape(image_count, token_count, model_width)
    output_rows = stream.astype(jnp.float32) + update
    return (output_rows, (normed, mixed_rows))

def reassemble_map(features, weight):
    flat_rows = features.reshape(-1, features.shape[-1]).astype(jnp.bfloat16)
    return jnp.dot(flat_rows, weight, preferred_element_type=jnp.float32).astype(jnp.bfloat16)

def head_rest(projected, top_projected, merging, predict, pixel_index, point_mask, point_depth):
    merged = top_projected.astype(jnp.float32)
    for hook_slot in range(len(projected) - 1, -1, -1):
        activated = jax.nn.silu(merged).astype(jnp.bfloat16)
        merged = projected[hook_slot].astype(jnp.float32) + jnp.dot(activated, merging[hook_slot], preferred_element_type=jnp.float32)
    activated = jax.nn.silu(merged).astype(jnp.bfloat16)
    depth_rows = jnp.dot(activated, predict, preferred_element_type=jnp.float32)
    depth_map = depth_rows.reshape(pixel_index.shape[0], pixel_index.shape[1], -1)
    picked = jnp.take_along_axis(depth_map, pixel_index, axis=2)
    valid_mask = point_mask.astype(jnp.float32)
    valid_count = lax.optimization_barrier(jnp.sum(valid_mask, axis=2))
    misfit = (picked - point_depth) * valid_mask
    return jnp.sum(lax.optimization_barrier(jnp.sum(misfit * misfit, axis=2)) / valid_count)

def head_loss(features, reassemble, merging, predict, pixel_index, point_mask, point_depth):
    hook_count = len(features) - 1
    projected = tuple((reassemble_map(features[hook_slot], reassemble[hook_slot]) for hook_slot in range(hook_count)))
    top_projected = reassemble_map(features[hook_count], reassemble[hook_count])
    return head_rest(projected, top_projected, merging, predict, pixel_index, point_mask, point_depth)

def reference(tokens, pixel_index, point_mask, point_depth, hook_section, w_query, w_key, w_value, w_output, reassemble, merging, predict):
    zero_nudges = jnp.zeros((3, 1, 1), jnp.bfloat16)
    all_weights = (w_query, w_key, w_value, w_output, reassemble, merging, predict)

    def block_loss(weights, image_block):
        block_tokens, block_index, block_mask, block_depth = image_block
        stream = block_tokens.reshape(MB * IMG_DEV, L, D).astype(jnp.float32)

        def section_step(carried, section_weights):
            output_rows = attention_layer(carried, section_weights[0], section_weights[1], section_weights[2], section_weights[3], zero_nudges)[0]
            return (output_rows, output_rows)
        top_feature, stacked = lax.scan(section_step, stream, (weights[0], weights[1], weights[2], weights[3]))
        hooked = tuple((lax.dynamic_index_in_dim(stacked, hook_section[hook_slot], 0, keepdims=False) for hook_slot in range(NHOOK)))
        return head_loss(hooked + (top_feature,), weights[4], weights[5], weights[6], block_index, block_mask, block_depth)

    def per_block(running, block_number):
        start_image = (block_number * IMG_DEV).astype(jnp.int32)
        image_block = tuple((lax.dynamic_slice_in_dim(array_item, start_image, IMG_DEV, 1) for array_item in (tokens, pixel_index, point_mask, point_depth)))
        loss_value, pullback = jax.vjp(lambda weights: block_loss(weights, image_block), all_weights)
        block_grads = pullback(jnp.ones((), jnp.float32))[0]
        return (tuple((running_sum + piece_grad.astype(jnp.float32) for running_sum, piece_grad in zip(running, block_grads))), None)
    zero_grads = tuple((jnp.zeros(array_item.shape, jnp.float32) for array_item in all_weights))
    running, unused = lax.scan(per_block, zero_grads, jnp.arange(N_DP, dtype=jnp.int32))
    return (running[0].astype(jnp.bfloat16), running[1].astype(jnp.bfloat16), running[2].astype(jnp.bfloat16), running[3].astype(jnp.bfloat16), running[4], running[5], running[6])
```

```python
import functools
import math

import jax
import jax.numpy as jnp
from jax import lax
from jax.experimental import pallas as pl
from jax.experimental.pallas import tpu as pltpu
from jax.sharding import PartitionSpec as P

HEADS = 13
NHOOK = 4
EPS = 1e-06

F32 = jnp.float32
BF16 = jnp.bfloat16


def mm(a, b):
    return lax.dot_general(a, b, (((1,), (0,)), ((), ())), preferred_element_type=F32)


def mm_nt(a, b):
    return lax.dot_general(a, b, (((1,), (1,)), ((), ())), preferred_element_type=F32)


def mm_tn(a, b):
    return lax.dot_general(a, b, (((0,), (0,)), ((), ())), preferred_element_type=F32)


def exact_mm(a, b, dims):
    return lax.dot_general(
        a, b, (dims, ((), ())), preferred_element_type=F32, precision=lax.Precision.HIGHEST
    )


def sigmoid(v):
    return 1.0 / (1.0 + jnp.exp(-v))


def body(
    sections, dps,
    tok, pix, msk, dep, hook, wq, wk, wv, wo, rea, mer, pred,
    normed_g, mixed_g, dq_g, dk_g, dv_g, cot_g, feat_g, dr_g, hd_g,
    x_st, q_st, k_st, v_st, p_st, xr_in, xr_out, gr_in, gr_out, top_g, dd_st, x_cot,
    fsend, frecv, bsend, brecv, gsend, grecv,
):
    micro, rows, width = tok.shape
    inner = wq.shape[1]
    hw = inner // HEADS
    feats = rea.shape[1]
    pixels = pred.shape[1]
    points = pix.shape[2]
    pad = xr_in.shape[2] - NHOOK * feats
    big = HEADS * rows
    s = lax.axis_index("section")
    last = sections - 1

    d = lax.axis_index("dp")
    normed_o, mixed_o, dq_o, dk_o, dv_o, cot_o, feat_o, dr_o, hd_o = [
        ref.at[d]
        for ref in (normed_g, mixed_g, dq_g, dk_g, dv_g, cot_g, feat_g, dr_g, hd_g)
    ]
    barrier = pltpu.get_barrier_semaphore()
    for hop in range(1, dps):
        pl.semaphore_signal(barrier, inc=1, device_id={"dp": lax.rem(d + hop, dps)},
                            device_id_type=pl.DeviceIdType.MESH)

    @pl.when(s > 0)
    def _():
        pl.semaphore_signal(barrier, inc=1, device_id={"section": s - 1},
                            device_id_type=pl.DeviceIdType.MESH)

    @pl.when(s < last)
    def _():
        pl.semaphore_signal(barrier, inc=1, device_id={"section": s + 1},
                            device_id_type=pl.DeviceIdType.MESH)

    pl.semaphore_wait(barrier, dps - 1 + jnp.where(s > 0, 1, 0) + jnp.where(s < last, 1, 0))

    owned = [hook[j] == s for j in range(NHOOK)]

    def fwd_copy(m):
        return pltpu.make_async_remote_copy(
            src_ref=xr_out.at[m], dst_ref=xr_in.at[m],
            send_sem=fsend.at[m], recv_sem=frecv.at[m],
            device_id={"section": s + 1}, device_id_type=pl.DeviceIdType.MESH)

    def bwd_copy(m):
        return pltpu.make_async_remote_copy(
            src_ref=gr_out.at[m], dst_ref=gr_in.at[m],
            send_sem=bsend.at[m], recv_sem=brecv.at[m],
            device_id={"section": s - 1}, device_id_type=pl.DeviceIdType.MESH)

    def spread_copy(place, ref, m, hop):
        return pltpu.make_async_remote_copy(
            src_ref=ref.at[d, m], dst_ref=ref.at[d, m],
            send_sem=gsend.at[place, m, hop], recv_sem=grecv.at[place, m, hop],
            device_id={"dp": lax.rem(d + hop, dps)}, device_id_type=pl.DeviceIdType.MESH)

    early = ((0, normed_g), (1, mixed_g), (2, feat_g))
    late = ((3, cot_g), (4, dq_g), (5, dk_g), (6, dv_g), (7, dr_g))
    heads = ((8, hd_g),)

    def send_group(group, m):
        for place, ref in group:
            for hop in range(1, dps):
                spread_copy(place, ref, m, hop).start()

    def wait_group(group, m):
        for place, ref in group:
            for hop in range(1, dps):
                spread_copy(place, ref, m, hop).wait()

    def head_mask():
        row_head = lax.broadcasted_iota(jnp.int32, (HEADS, rows, inner), 0)
        col = lax.broadcasted_iota(jnp.int32, (HEADS, rows, inner), 2)
        lo = row_head * hw
        return ((col >= lo) & (col < lo + hw)).reshape(big, inner)

    def spread(a, mask):
        tiled = jnp.broadcast_to(a[None], (HEADS,) + a.shape).reshape(big, inner)
        return jnp.where(mask, tiled, 0.0).astype(BF16)

    def gathered(a, mask):
        return jnp.sum(jnp.where(mask, a, 0.0).reshape(HEADS, rows, inner), axis=0)

    def forward(m, carry):
        @pl.when(s > 0)
        def _():
            fwd_copy(m).wait_recv()

        first = s == 0
        arrived = xr_in[m]
        x = jnp.where(first, tok[m].astype(F32), arrived[:, :width].astype(F32))
        x_st[m] = x
        inv = lax.rsqrt(jnp.mean(x * x, axis=-1, keepdims=True) + EPS)
        normed = (x * inv).astype(BF16)
        normed_o[m] = normed
        q = mm(normed, wq[...])
        k = mm(normed, wk[...]).astype(BF16)
        v = mm(normed, wv[...]).astype(BF16)
        q_st[m] = q.astype(BF16)
        k_st[m] = k
        v_st[m] = v
        mask = head_mask()
        scores = mm_nt(spread(q, mask), k) * (1.0 / math.sqrt(hw))
        top = jnp.max(scores, axis=-1, keepdims=True)
        e = jnp.exp(scores - top)
        p = e / jnp.sum(e, axis=-1, keepdims=True)
        p_st[m] = p
        mixed = gathered(mm(p.astype(BF16), v), mask).astype(BF16)
        mixed_o[m] = mixed
        y = x + mm(mixed, wo[...])
        feat = y.astype(BF16)
        feat_o[m] = feat
        xr_out[m, :, :width] = feat
        for j in range(NHOOK):
            before = arrived[:, pad + j * feats:pad + (j + 1) * feats].astype(F32)
            mine = mm_nt(feat, rea[j])
            xr_out[m, :, pad + j * feats:pad + (j + 1) * feats] = jnp.where(
                owned[j], mine, before).astype(BF16)

        @pl.when(s < last)
        def _():
            fwd_copy(m).start()

        send_group(early, m)
        return carry

    lax.fori_loop(0, micro, forward, 0)

    @pl.when(s < last)
    def _():
        hd_g[...] = jnp.zeros_like(hd_g)
        dr_o[:, :, NHOOK * feats:] = jnp.zeros((micro, rows, feats), BF16)

    @pl.when(s == last)
    def _():
        total = micro * rows
        r_all = xr_in[:, :, pad:].reshape(total, NHOOK * feats)
        r = [r_all[:, j * feats:(j + 1) * feats].astype(F32) for j in range(NHOOK)]
        r_top = mm_nt(feat_o[...].reshape(total, width), rea[NHOOK]).astype(BF16).astype(F32)
        merged = [None] * NHOOK + [r_top]
        gate = [None] * (NHOOK + 1)
        act = [None] * (NHOOK + 1)
        for j in range(NHOOK, -1, -1):
            gate[j] = sigmoid(merged[j])
            act[j] = (merged[j] * gate[j]).astype(BF16)
            if j > 0:
                merged[j - 1] = r[j - 1] + mm_nt(act[j], mer[j - 1])
        depth = mm(act[0], pred[...])
        edge = lax.broadcasted_iota(jnp.int32, (rows, points), 0) * pixels
        place = lax.broadcasted_iota(jnp.int32, (pixels, points), 0)
        for m in range(micro):
            where = jnp.broadcast_to(pix[m], (rows, points))
            over = where >= edge
            token_hot = (over & (where < edge + pixels)).astype(F32)
            token_id = jnp.sum(over.astype(F32), axis=0, keepdims=True).astype(jnp.int32) - 1
            pix_hot = (place == (pix[m] - token_id * pixels)).astype(F32)
            spot = exact_mm(depth[m * rows:(m + 1) * rows], pix_hot, ((1,), (0,)))
            picked = jnp.sum(spot * token_hot, axis=0, keepdims=True)
            valid = msk[m].astype(F32)
            count = jnp.sum(valid, axis=1, keepdims=True)
            slope = 2.0 * (picked - dep[m]) * valid * valid / count
            dd_st[m * rows:(m + 1) * rows, :] = exact_mm(token_hot * slope, pix_hot, ((1,), (1,)))
        dd = dd_st[...].astype(BF16)
        hd_o[:, :, (2 * NHOOK + 1) * feats:] = dd.reshape(micro, rows, pixels)
        for j in range(NHOOK + 1):
            hd_o[:, :, (NHOOK + j) * feats:(NHOOK + j + 1) * feats] = act[j].reshape(
                micro, rows, feats)
        d_act = mm_nt(dd, pred[...]).astype(BF16).astype(F32)
        for j in range(NHOOK + 1):
            d_merged = d_act * (gate[j] * (1.0 + merged[j] * (1.0 - gate[j])))
            d_low = d_merged.astype(BF16)
            if j < NHOOK:
                gr_out[:, :, pad + j * feats:pad + (j + 1) * feats] = d_low.reshape(
                    micro, rows, feats)
                hd_o[:, :, j * feats:(j + 1) * feats] = d_low.reshape(micro, rows, feats)
                d_act = mm(d_low, mer[j]).astype(BF16).astype(F32)
                dr_o[:, :, j * feats:(j + 1) * feats] = jnp.zeros((micro, rows, feats), BF16)
            else:
                dr_o[:, :, j * feats:(j + 1) * feats] = d_low.reshape(micro, rows, feats)
                top_g[...] = mm(d_low, rea[NHOOK]).reshape(micro, rows, width).astype(BF16)

        for m in range(micro):
            send_group(heads, m)

    def backward(m, carry):
        @pl.when(s < last)
        def _():
            bwd_copy(m).wait_recv()
            arrived = gr_in[m]
            g = arrived[:, :width].astype(F32)
            for j in range(NHOOK):
                part = arrived[:, pad + j * feats:pad + (j + 1) * feats].astype(F32)
                gr_out[m, :, pad + j * feats:pad + (j + 1) * feats] = part.astype(BF16)
                kept = jnp.where(owned[j], part, 0.0).astype(BF16)
                dr_o[m, :, j * feats:(j + 1) * feats] = kept
                g = g + mm(kept, rea[j])
            x_cot[...] = g

        @pl.when(s == last)
        def _():
            x_cot[...] = top_g[m].astype(F32)

        g = x_cot[...]
        g_low = g.astype(BF16)
        cot_o[m] = g_low
        d_mixed = mm_nt(g_low, wo[...])
        mask = head_mask()
        q_big = spread(q_st[m].astype(F32), mask)
        dm_big = spread(d_mixed, mask)
        p = p_st[m]
        dp = mm_nt(dm_big, v_st[m]).astype(BF16).astype(F32)
        ds = (p * (dp - jnp.sum(dp * p, axis=-1, keepdims=True)) * (1.0 / math.sqrt(hw)))
        ds = ds.astype(BF16)
        dv = mm_tn(p.astype(BF16), dm_big).astype(BF16)
        dk = mm_tn(ds, q_big).astype(BF16)
        dq = gathered(mm(ds, k_st[m]), mask).astype(BF16)
        dq_o[m] = dq
        dk_o[m] = dk
        dv_o[m] = dv

        @pl.when(s > 0)
        def _():
            dn = mm_nt(dq, wq[...]) + mm_nt(dk, wk[...]) + mm_nt(dv, wv[...])
            x = x_st[m]
            inv = lax.rsqrt(jnp.mean(x * x, axis=-1, keepdims=True) + EPS)
            along = jnp.mean(dn * x, axis=-1, keepdims=True)
            dx = x_cot[...] + inv * dn - x * (inv * inv * inv * along)
            gr_out[m, :, :width] = dx.astype(BF16)
            bwd_copy(m).start()

        send_group(late, m)
        return carry

    lax.fori_loop(0, micro, backward, 0)

    @pl.when(s < last)
    def _():
        for m in range(micro):
            fwd_copy(m).wait_send()

    @pl.when(s == last)
    def _():
        for m in range(micro):
            wait_group(heads, m)

    @pl.when(s > 0)
    def _():
        for m in range(micro):
            bwd_copy(m).wait_send()

    def settle(m, carry):
        wait_group(early, m)
        wait_group(late, m)
        return carry

    lax.fori_loop(0, micro, settle, 0)


def pipeline(sections, dps, tok, pix, msk, dep, hook, wq, wk, wv, wo, rea, mer, pred):
    micro, rows, width = tok.shape
    inner = wq.shape[1]
    feats = rea.shape[1]
    pixels = pred.shape[1]
    pad = -(-width // 128) * 128
    wide = pad + NHOOK * feats
    vm = pl.BlockSpec(memory_space=pltpu.VMEM)
    sm = pl.BlockSpec(memory_space=pltpu.SMEM)

    def low(*shape):
        return jax.ShapeDtypeStruct((dps,) + shape, BF16)

    return pl.pallas_call(
        functools.partial(body, sections, dps),
        out_shape=(
            low(micro, rows, width), low(micro, rows, inner),
            low(micro, rows, inner), low(micro, rows, inner), low(micro, rows, inner),
            low(micro, rows, width), low(micro, rows, width),
            low(micro, rows, (NHOOK + 1) * feats),
            low(micro, rows, (2 * NHOOK + 1) * feats + pixels),
        ),
        in_specs=[vm, vm, vm, vm, sm] + [vm] * 7,
        out_specs=tuple([vm] * 9),
        scratch_shapes=[
            pltpu.VMEM((micro, rows, width), F32),
            pltpu.VMEM((micro, rows, inner), BF16),
            pltpu.VMEM((micro, rows, inner), BF16),
            pltpu.VMEM((micro, rows, inner), BF16),
            pltpu.VMEM((micro, HEADS * rows, rows), F32),
            pltpu.VMEM((micro, rows, wide), BF16),
            pltpu.VMEM((micro, rows, wide), BF16),
            pltpu.VMEM((micro, rows, wide), BF16),
            pltpu.VMEM((micro, rows, wide), BF16),
            pltpu.VMEM((micro, rows, width), BF16),
            pltpu.VMEM((micro * rows, pixels), F32),
            pltpu.VMEM((rows, width), F32),
            pltpu.SemaphoreType.DMA((micro,)),
            pltpu.SemaphoreType.DMA((micro,)),
            pltpu.SemaphoreType.DMA((micro,)),
            pltpu.SemaphoreType.DMA((micro,)),
            pltpu.SemaphoreType.DMA((9, micro, dps)),
            pltpu.SemaphoreType.DMA((9, micro, dps)),
        ],
        compiler_params=pltpu.CompilerParams(
            collective_id=0, has_side_effects=True, vmem_limit_bytes=56 * 1024 * 1024
        ),
    )(tok, pix, msk, dep, hook, wq, wk, wv, wo, rea, mer, pred)


def on_device(
    tokens, pixel_index, point_mask, point_depth, hook_section,
    w_query, w_key, w_value, w_output, reassemble, merging, predict,
):
    sections = lax.axis_size("section")
    dps = lax.axis_size("dp")
    d_index = lax.axis_index("dp")
    micro, images, tokens_in, width = tokens.shape
    rows = images * tokens_in
    points = pixel_index.shape[2]
    inner = w_query.shape[2]
    both = ("section", "dp")

    def whole(local):
        turned = jnp.swapaxes(local, 1, 2)
        every = lax.all_gather(turned, both, axis=0)
        return jnp.swapaxes(every, 0, 1).reshape(local.shape[0], -1, local.shape[1])

    rea = whole(reassemble)
    mer = whole(merging)
    pred = lax.all_gather(predict, both, axis=0, tiled=True)
    feats = rea.shape[1]

    normed, mixed, dq, dk, dv, cot, feat, dr, hd = pipeline(
        sections, dps,
        tokens.reshape(micro, rows, width),
        pixel_index.reshape(micro, 1, points),
        point_mask.reshape(micro, 1, points),
        point_depth.reshape(micro, 1, points),
        hook_section,
        w_query[0], w_key[0], w_value[0], w_output[0], rea, mer, pred,
    )
    total = micro * rows

    def dp_rows(a):
        return a.reshape(dps * total, a.shape[3])

    def own(a, size):
        return lax.dynamic_slice_in_dim(a, d_index * size, size, 1)

    normed_own = own(dp_rows(normed), width // dps)
    mixed_own = own(dp_rows(mixed), inner // dps)
    grad_query = mm_tn(normed_own, dp_rows(dq)).astype(BF16)
    grad_key = mm_tn(normed_own, dp_rows(dk)).astype(BF16)
    grad_value = mm_tn(normed_own, dp_rows(dv)).astype(BF16)
    grad_output = mm_tn(mixed_own, dp_rows(cot)).astype(BF16)

    piece = feats // (sections * dps)

    def columns(a, count):
        cut = a.reshape(dps * total, count, sections, dps, piece)
        return lax.dynamic_index_in_dim(cut, d_index, 3, keepdims=False)

    dr_own = columns(dp_rows(dr), NHOOK + 1).transpose(0, 2, 1, 3).reshape(dps * total, -1)
    part_rea = mm_tn(dr_own, dp_rows(feat)).reshape(sections, -1)
    hd_rows = dp_rows(hd)
    d_low = columns(hd_rows[:, :NHOOK * feats], NHOOK)
    acts = hd_rows[:, NHOOK * feats:(2 * NHOOK + 1) * feats].reshape(-1, NHOOK + 1, feats)
    part_mer = jnp.einsum("njsc,njf->sjcf", d_low, acts[:, 1:], preferred_element_type=F32)
    act_own = columns(acts[:, 0], 1).reshape(dps * total, sections * piece)
    part_pred = mm_tn(act_own, hd_rows[:, (2 * NHOOK + 1) * feats:])
    sent = jnp.concatenate(
        [part_rea, part_mer.reshape(sections, -1), part_pred.reshape(sections, -1)], axis=1)
    sent = jnp.pad(sent, ((0, 0), (0, -sent.shape[1] % 1024))).reshape(sections, -1, 128)
    mine = lax.psum_scatter(sent, "section", scatter_dimension=0, tiled=False).reshape(-1)
    cut_rea = (NHOOK + 1) * piece * width
    cut_mer = cut_rea + NHOOK * piece * feats
    grad_reassemble = mine[:cut_rea].reshape(NHOOK + 1, piece, width).swapaxes(1, 2)
    grad_merging = mine[cut_rea:cut_mer].reshape(NHOOK, piece, feats).swapaxes(1, 2)
    grad_predict = mine[cut_mer:cut_mer + piece * pred.shape[1]].reshape(piece, -1)
    return (
        grad_query[None], grad_key[None], grad_value[None], grad_output[None],
        grad_reassemble, grad_merging, grad_predict,
    )


def solution(mesh):
    placed = (
        P(None, ("group", "dp"), None, None),
        P(None, ("group", "dp"), None),
        P(None, ("group", "dp"), None),
        P(None, ("group", "dp"), None),
        P(),
        P("section", None, None),
        P("section", None, None),
        P("section", None, None),
        P("section", None, None),
        P(None, None, ("section", "dp")),
        P(None, None, ("section", "dp")),
        P(("section", "dp"), None),
    )
    return jax.shard_map(
        on_device,
        mesh=mesh,
        in_specs=placed,
        out_specs=(
            P(("group", "section"), "dp", None),
            P(("group", "section"), "dp", None),
            P(("group", "section"), "dp", None),
            P(("group", "section"), "dp", None),
            P("group", None, ("section", "dp")),
            P("group", None, ("section", "dp")),
            P(("group", "section", "dp"), None),
        ),
        check_vma=False,
    )
```

```python
import functools
import math

import jax
import jax.numpy as jnp
from jax import lax
from jax.experimental import pallas as pl
from jax.experimental.pallas import tpu as pltpu
from jax.sharding import PartitionSpec as P

HEADS = 13
NHOOK = 4
EPS = 1e-06

F32 = jnp.float32
BF16 = jnp.bfloat16


def mm(a, b):
    return lax.dot_general(a, b, (((1,), (0,)), ((), ())), preferred_element_type=F32)


def mm_nt(a, b):
    return lax.dot_general(a, b, (((1,), (1,)), ((), ())), preferred_element_type=F32)


def mm_tn(a, b):
    return lax.dot_general(a, b, (((0,), (0,)), ((), ())), preferred_element_type=F32)


def exact_mm(a, b, dims):
    return lax.dot_general(
        a, b, (dims, ((), ())), preferred_element_type=F32, precision=lax.Precision.HIGHEST
    )


def sigmoid(v):
    return 1.0 / (1.0 + jnp.exp(-v))


def body(
    sections, dps,
    tok, pix, msk, dep, hook, wq, wk, wv, wo, rea, mer, pred,
    normed_g, mixed_g, dq_g, dk_g, dv_g, cot_g, feat_g, dr_g, hd_g,
    x_st, q_st, k_st, v_st, p_st, xr_in, xr_out, gr_in, gr_out, top_g, dd_st, x_cot,
    fsend, frecv, bsend, brecv, gsend, grecv,
):
    micro, rows, width = tok.shape
    inner = wq.shape[1]
    hw = inner // HEADS
    feats = rea.shape[1]
    pixels = pred.shape[1]
    points = pix.shape[2]
    pad = xr_in.shape[2] - NHOOK * feats
    big = HEADS * rows
    s = lax.axis_index("section")
    last = sections - 1

    d = lax.axis_index("dp")
    normed_o, mixed_o, dq_o, dk_o, dv_o, cot_o, feat_o, dr_o, hd_o = [
        ref.at[d]
        for ref in (normed_g, mixed_g, dq_g, dk_g, dv_g, cot_g, feat_g, dr_g, hd_g)
    ]
    barrier = pltpu.get_barrier_semaphore()
    for hop in range(1, dps):
        pl.semaphore_signal(barrier, inc=1, device_id={"dp": lax.rem(d + hop, dps)},
                            device_id_type=pl.DeviceIdType.MESH)

    @pl.when(s > 0)
    def _():
        pl.semaphore_signal(barrier, inc=1, device_id={"section": s - 1},
                            device_id_type=pl.DeviceIdType.MESH)

    @pl.when(s < last)
    def _():
        pl.semaphore_signal(barrier, inc=1, device_id={"section": s + 1},
                            device_id_type=pl.DeviceIdType.MESH)

    pl.semaphore_wait(barrier, dps - 1 + jnp.where(s > 0, 1, 0) + jnp.where(s < last, 1, 0))

    owned = [hook[j] == s for j in range(NHOOK)]

    def fwd_copy(m):
        return pltpu.make_async_remote_copy(
            src_ref=xr_out.at[m], dst_ref=xr_in.at[m],
            send_sem=fsend.at[m], recv_sem=frecv.at[m],
            device_id={"section": s + 1}, device_id_type=pl.DeviceIdType.MESH)

    def bwd_copy(m):
        return pltpu.make_async_remote_copy(
            src_ref=gr_out.at[m], dst_ref=gr_in.at[m],
            send_sem=bsend.at[m], recv_sem=brecv.at[m],
            device_id={"section": s - 1}, device_id_type=pl.DeviceIdType.MESH)

    mate = d + 1 - 2 * lax.rem(d, 2)

    def spread_copy(place, ref, m, hop):
        block = d if hop % 2 == 0 or hop == 1 else lax.rem(d + dps - hop + 1, dps)
        target = mate if hop % 2 == 1 else lax.rem(d + hop, dps)
        return pltpu.make_async_remote_copy(
            src_ref=ref.at[block, m], dst_ref=ref.at[block, m],
            send_sem=gsend.at[place, m, hop], recv_sem=grecv.at[place, m, hop],
            device_id={"dp": target}, device_id_type=pl.DeviceIdType.MESH)

    early = ((0, normed_g), (1, mixed_g), (2, feat_g))
    late = ((3, cot_g), (4, dq_g), (5, dk_g), (6, dv_g), (7, dr_g))
    heads = ((8, hd_g),)

    def send_group(group, m):
        for place, ref in group:
            for hop in [*range(2, dps, 2), 1]:
                spread_copy(place, ref, m, hop).start()

    def relay_group(group, m):
        for place, ref in group:
            for hop in range(2, dps, 2):
                spread_copy(place, ref, m, hop).wait_recv()
                spread_copy(place, ref, m, hop + 1).start()

    def wait_group(group, m):
        for place, ref in group:
            for hop in range(1, dps):
                if hop % 2 == 0:
                    spread_copy(place, ref, m, hop).wait_send()
                else:
                    spread_copy(place, ref, m, hop).wait()

    def head_mask():
        row_head = lax.broadcasted_iota(jnp.int32, (HEADS, rows, inner), 0)
        col = lax.broadcasted_iota(jnp.int32, (HEADS, rows, inner), 2)
        lo = row_head * hw
        return ((col >= lo) & (col < lo + hw)).reshape(big, inner)

    def spread(a, mask):
        tiled = jnp.broadcast_to(a[None], (HEADS,) + a.shape).reshape(big, inner)
        return jnp.where(mask, tiled, 0.0).astype(BF16)

    def gathered(a, mask):
        return jnp.sum(jnp.where(mask, a, 0.0).reshape(HEADS, rows, inner), axis=0)

    def forward(m, carry):
        @pl.when(s > 0)
        def _():
            fwd_copy(m).wait_recv()

        first = s == 0
        arrived = xr_in[m]
        x = jnp.where(first, tok[m].astype(F32), arrived[:, :width].astype(F32))
        x_st[m] = x
        inv = lax.rsqrt(jnp.mean(x * x, axis=-1, keepdims=True) + EPS)
        normed = (x * inv).astype(BF16)
        normed_o[m] = normed
        q = mm(normed, wq[...])
        k = mm(normed, wk[...]).astype(BF16)
        v = mm(normed, wv[...]).astype(BF16)
        q_st[m] = q.astype(BF16)
        k_st[m] = k
        v_st[m] = v
        mask = head_mask()
        scores = mm_nt(spread(q, mask), k) * (1.0 / math.sqrt(hw))
        top = jnp.max(scores, axis=-1, keepdims=True)
        e = jnp.exp(scores - top)
        p = e / jnp.sum(e, axis=-1, keepdims=True)
        p_st[m] = p
        mixed = gathered(mm(p.astype(BF16), v), mask).astype(BF16)
        mixed_o[m] = mixed
        y = x + mm(mixed, wo[...])
        feat = y.astype(BF16)
        feat_o[m] = feat
        xr_out[m, :, :width] = feat
        for j in range(NHOOK):
            before = arrived[:, pad + j * feats:pad + (j + 1) * feats].astype(F32)
            mine = mm_nt(feat, rea[j])
            xr_out[m, :, pad + j * feats:pad + (j + 1) * feats] = jnp.where(
                owned[j], mine, before).astype(BF16)

        @pl.when(s < last)
        def _():
            fwd_copy(m).start()

        send_group(early, m)
        return carry

    lax.fori_loop(0, micro, forward, 0)

    @pl.when(s < last)
    def _():
        hd_g[...] = jnp.zeros_like(hd_g)
        dr_o[:, :, NHOOK * feats:] = jnp.zeros((micro, rows, feats), BF16)

    @pl.when(s == last)
    def _():
        total = micro * rows
        r_all = xr_in[:, :, pad:].reshape(total, NHOOK * feats)
        r = [r_all[:, j * feats:(j + 1) * feats].astype(F32) for j in range(NHOOK)]
        r_top = mm_nt(feat_o[...].reshape(total, width), rea[NHOOK]).astype(BF16).astype(F32)
        merged = [None] * NHOOK + [r_top]
        gate = [None] * (NHOOK + 1)
        act = [None] * (NHOOK + 1)
        for j in range(NHOOK, -1, -1):
            gate[j] = sigmoid(merged[j])
            act[j] = (merged[j] * gate[j]).astype(BF16)
            if j > 0:
                merged[j - 1] = r[j - 1] + mm_nt(act[j], mer[j - 1])
        depth = mm(act[0], pred[...])
        edge = lax.broadcasted_iota(jnp.int32, (rows, points), 0) * pixels
        place = lax.broadcasted_iota(jnp.int32, (pixels, points), 0)
        for m in range(micro):
            where = jnp.broadcast_to(pix[m], (rows, points))
            over = where >= edge
            token_hot = (over & (where < edge + pixels)).astype(F32)
            token_id = jnp.sum(over.astype(F32), axis=0, keepdims=True).astype(jnp.int32) - 1
            pix_hot = (place == (pix[m] - token_id * pixels)).astype(F32)
            spot = exact_mm(depth[m * rows:(m + 1) * rows], pix_hot, ((1,), (0,)))
            picked = jnp.sum(spot * token_hot, axis=0, keepdims=True)
            valid = msk[m].astype(F32)
            count = jnp.sum(valid, axis=1, keepdims=True)
            slope = 2.0 * (picked - dep[m]) * valid * valid / count
            dd_st[m * rows:(m + 1) * rows, :] = exact_mm(token_hot * slope, pix_hot, ((1,), (1,)))
        dd = dd_st[...].astype(BF16)
        hd_o[:, :, (2 * NHOOK + 1) * feats:] = dd.reshape(micro, rows, pixels)
        for j in range(NHOOK + 1):
            hd_o[:, :, (NHOOK + j) * feats:(NHOOK + j + 1) * feats] = act[j].reshape(
                micro, rows, feats)
        d_act = mm_nt(dd, pred[...]).astype(BF16).astype(F32)
        for j in range(NHOOK + 1):
            d_merged = d_act * (gate[j] * (1.0 + merged[j] * (1.0 - gate[j])))
            d_low = d_merged.astype(BF16)
            if j < NHOOK:
                gr_out[:, :, pad + j * feats:pad + (j + 1) * feats] = d_low.reshape(
                    micro, rows, feats)
                hd_o[:, :, j * feats:(j + 1) * feats] = d_low.reshape(micro, rows, feats)
                d_act = mm(d_low, mer[j]).astype(BF16).astype(F32)
                dr_o[:, :, j * feats:(j + 1) * feats] = jnp.zeros((micro, rows, feats), BF16)
            else:
                dr_o[:, :, j * feats:(j + 1) * feats] = d_low.reshape(micro, rows, feats)
                top_g[...] = mm(d_low, rea[NHOOK]).reshape(micro, rows, width).astype(BF16)

        for m in range(micro):
            send_group(heads, m)

    def backward(m, carry):
        @pl.when(s < last)
        def _():
            bwd_copy(m).wait_recv()
            arrived = gr_in[m]
            g = arrived[:, :width].astype(F32)
            for j in range(NHOOK):
                part = arrived[:, pad + j * feats:pad + (j + 1) * feats].astype(F32)
                gr_out[m, :, pad + j * feats:pad + (j + 1) * feats] = part.astype(BF16)
                kept = jnp.where(owned[j], part, 0.0).astype(BF16)
                dr_o[m, :, j * feats:(j + 1) * feats] = kept
                g = g + mm(kept, rea[j])
            x_cot[...] = g

        @pl.when(s == last)
        def _():
            x_cot[...] = top_g[m].astype(F32)

        g = x_cot[...]
        g_low = g.astype(BF16)
        cot_o[m] = g_low
        d_mixed = mm_nt(g_low, wo[...])
        mask = head_mask()
        q_big = spread(q_st[m].astype(F32), mask)
        dm_big = spread(d_mixed, mask)
        p = p_st[m]
        dp = mm_nt(dm_big, v_st[m]).astype(BF16).astype(F32)
        ds = (p * (dp - jnp.sum(dp * p, axis=-1, keepdims=True)) * (1.0 / math.sqrt(hw)))
        ds = ds.astype(BF16)
        dv = mm_tn(p.astype(BF16), dm_big).astype(BF16)
        dk = mm_tn(ds, q_big).astype(BF16)
        dq = gathered(mm(ds, k_st[m]), mask).astype(BF16)
        dq_o[m] = dq
        dk_o[m] = dk
        dv_o[m] = dv

        @pl.when(s > 0)
        def _():
            dn = mm_nt(dq, wq[...]) + mm_nt(dk, wk[...]) + mm_nt(dv, wv[...])
            x = x_st[m]
            inv = lax.rsqrt(jnp.mean(x * x, axis=-1, keepdims=True) + EPS)
            along = jnp.mean(dn * x, axis=-1, keepdims=True)
            dx = x_cot[...] + inv * dn - x * (inv * inv * inv * along)
            gr_out[m, :, :width] = dx.astype(BF16)
            bwd_copy(m).start()

        send_group(late, m)
        relay_group(early, m)

        @pl.when(m > 0)
        def _():
            relay_group(late, m - 1)

        return carry

    lax.fori_loop(0, micro, backward, 0)
    relay_group(late, micro - 1)

    @pl.when(s == last)
    def _():
        for m in range(micro):
            relay_group(heads, m)

    @pl.when(s < last)
    def _():
        for m in range(micro):
            fwd_copy(m).wait_send()

    @pl.when(s == last)
    def _():
        for m in range(micro):
            wait_group(heads, m)

    @pl.when(s > 0)
    def _():
        for m in range(micro):
            bwd_copy(m).wait_send()

    def settle(m, carry):
        wait_group(early, m)
        wait_group(late, m)
        return carry

    lax.fori_loop(0, micro, settle, 0)


def pipeline(sections, dps, tok, pix, msk, dep, hook, wq, wk, wv, wo, rea, mer, pred):
    micro, rows, width = tok.shape
    inner = wq.shape[1]
    feats = rea.shape[1]
    pixels = pred.shape[1]
    pad = -(-width // 128) * 128
    wide = pad + NHOOK * feats
    vm = pl.BlockSpec(memory_space=pltpu.VMEM)
    sm = pl.BlockSpec(memory_space=pltpu.SMEM)

    def low(*shape):
        return jax.ShapeDtypeStruct((dps,) + shape, BF16)

    return pl.pallas_call(
        functools.partial(body, sections, dps),
        out_shape=(
            low(micro, rows, width), low(micro, rows, inner),
            low(micro, rows, inner), low(micro, rows, inner), low(micro, rows, inner),
            low(micro, rows, width), low(micro, rows, width),
            low(micro, rows, (NHOOK + 1) * feats),
            low(micro, rows, (2 * NHOOK + 1) * feats + pixels),
        ),
        in_specs=[vm, vm, vm, vm, sm] + [vm] * 7,
        out_specs=tuple([vm] * 9),
        scratch_shapes=[
            pltpu.VMEM((micro, rows, width), F32),
            pltpu.VMEM((micro, rows, inner), BF16),
            pltpu.VMEM((micro, rows, inner), BF16),
            pltpu.VMEM((micro, rows, inner), BF16),
            pltpu.VMEM((micro, HEADS * rows, rows), F32),
            pltpu.VMEM((micro, rows, wide), BF16),
            pltpu.VMEM((micro, rows, wide), BF16),
            pltpu.VMEM((micro, rows, wide), BF16),
            pltpu.VMEM((micro, rows, wide), BF16),
            pltpu.VMEM((micro, rows, width), BF16),
            pltpu.VMEM((micro * rows, pixels), F32),
            pltpu.VMEM((rows, width), F32),
            pltpu.SemaphoreType.DMA((micro,)),
            pltpu.SemaphoreType.DMA((micro,)),
            pltpu.SemaphoreType.DMA((micro,)),
            pltpu.SemaphoreType.DMA((micro,)),
            pltpu.SemaphoreType.DMA((9, micro, dps)),
            pltpu.SemaphoreType.DMA((9, micro, dps)),
        ],
        compiler_params=pltpu.CompilerParams(
            collective_id=0, has_side_effects=True, vmem_limit_bytes=56 * 1024 * 1024
        ),
    )(tok, pix, msk, dep, hook, wq, wk, wv, wo, rea, mer, pred)


def on_device(
    tokens, pixel_index, point_mask, point_depth, hook_section,
    w_query, w_key, w_value, w_output, reassemble, merging, predict,
):
    sections = lax.axis_size("section")
    dps = lax.axis_size("dp")
    d_index = lax.axis_index("dp")
    micro, images, tokens_in, width = tokens.shape
    rows = images * tokens_in
    points = pixel_index.shape[2]
    inner = w_query.shape[2]
    both = ("section", "dp")

    def whole(local):
        turned = jnp.swapaxes(local, 1, 2)
        every = lax.all_gather(turned, both, axis=0)
        return jnp.swapaxes(every, 0, 1).reshape(local.shape[0], -1, local.shape[1])

    rea = whole(reassemble)
    mer = whole(merging)
    pred = lax.all_gather(predict, both, axis=0, tiled=True)
    feats = rea.shape[1]

    normed, mixed, dq, dk, dv, cot, feat, dr, hd = pipeline(
        sections, dps,
        tokens.reshape(micro, rows, width),
        pixel_index.reshape(micro, 1, points),
        point_mask.reshape(micro, 1, points),
        point_depth.reshape(micro, 1, points),
        hook_section,
        w_query[0], w_key[0], w_value[0], w_output[0], rea, mer, pred,
    )
    total = micro * rows

    def dp_rows(a):
        return a.reshape(dps * total, a.shape[3])

    def own(a, size):
        return lax.dynamic_slice_in_dim(a, d_index * size, size, 1)

    normed_own = own(dp_rows(normed), width // dps)
    mixed_own = own(dp_rows(mixed), inner // dps)
    grad_query = mm_tn(normed_own, dp_rows(dq)).astype(BF16)
    grad_key = mm_tn(normed_own, dp_rows(dk)).astype(BF16)
    grad_value = mm_tn(normed_own, dp_rows(dv)).astype(BF16)
    grad_output = mm_tn(mixed_own, dp_rows(cot)).astype(BF16)

    piece = feats // (sections * dps)

    def columns(a, count):
        cut = a.reshape(dps * total, count, sections, dps, piece)
        return lax.dynamic_index_in_dim(cut, d_index, 3, keepdims=False)

    dr_own = columns(dp_rows(dr), NHOOK + 1).transpose(0, 2, 1, 3).reshape(dps * total, -1)
    part_rea = mm_tn(dr_own, dp_rows(feat)).reshape(sections, -1)
    hd_rows = dp_rows(hd)
    d_low = columns(hd_rows[:, :NHOOK * feats], NHOOK)
    acts = hd_rows[:, NHOOK * feats:(2 * NHOOK + 1) * feats].reshape(-1, NHOOK + 1, feats)
    part_mer = jnp.einsum("njsc,njf->sjcf", d_low, acts[:, 1:], preferred_element_type=F32)
    act_own = columns(acts[:, 0], 1).reshape(dps * total, sections * piece)
    part_pred = mm_tn(act_own, hd_rows[:, (2 * NHOOK + 1) * feats:])
    sent = jnp.concatenate(
        [part_rea, part_mer.reshape(sections, -1), part_pred.reshape(sections, -1)], axis=1)
    sent = jnp.pad(sent, ((0, 0), (0, -sent.shape[1] % 1024))).reshape(sections, -1, 128)
    mine = lax.psum_scatter(sent, "section", scatter_dimension=0, tiled=False).reshape(-1)
    cut_rea = (NHOOK + 1) * piece * width
    cut_mer = cut_rea + NHOOK * piece * feats
    grad_reassemble = mine[:cut_rea].reshape(NHOOK + 1, piece, width).swapaxes(1, 2)
    grad_merging = mine[cut_rea:cut_mer].reshape(NHOOK, piece, feats).swapaxes(1, 2)
    grad_predict = mine[cut_mer:cut_mer + piece * pred.shape[1]].reshape(piece, -1)
    return (
        grad_query[None], grad_key[None], grad_value[None], grad_output[None],
        grad_reassemble, grad_merging, grad_predict,
    )


def solution(mesh):
    placed = (
        P(None, ("group", "dp"), None, None),
        P(None, ("group", "dp"), None),
        P(None, ("group", "dp"), None),
        P(None, ("group", "dp"), None),
        P(),
        P("section", None, None),
        P("section", None, None),
        P("section", None, None),
        P("section", None, None),
        P(None, None, ("section", "dp")),
        P(None, None, ("section", "dp")),
        P(("section", "dp"), None),
    )
    return jax.shard_map(
        on_device,
        mesh=mesh,
        in_specs=placed,
        out_specs=(
            P(("group", "section"), "dp", None),
            P(("group", "section"), "dp", None),
            P(("group", "section"), "dp", None),
            P(("group", "section"), "dp", None),
            P("group", None, ("section", "dp")),
            P("group", None, ("section", "dp")),
            P(("group", "section", "dp"), None),
        ),
        check_vma=False,
    )
```
